512 devices in a mesh: stream: 32 (over z, core), gy: 4 (over y), gz: 4 (over x).
Axes of the slice: x: 4, y: 4, z: 16, core: 2. Of those that a mesh axis runs over, the one named last changes fastest.
Arguments:
- right_side: bfloat16 [32, 4, 4, 625, 768], P('stream', 'gy', 'gz'), may hold values from -6 to 6
- inverse: bfloat16 [32, 4, 4, 625, 625], P('stream', 'gy', 'gz'), may hold values from -0.3 to 1.3
- coupling: bfloat16 [32, 4, 4, 6, 625, 125], P('stream', 'gy', 'gz'), may hold values from -0.2593839 to 0.2593839
- initial_guess: bfloat16 [32, 4, 4, 625, 768], P('stream', 'gy', 'gz'), may hold values from -6 to 6
- face_order: int32 [32, 4, 4, 6, 125], P('stream', 'gy', 'gz'), may hold values from 0 to 124, each once within a row
Outputs:
- updated: bfloat16 [32, 4, 4, 625, 768], P('stream', 'gy', 'gz')
The draws below stay inside these ranges and needn't reach their ends.
Inputs may be any that keep to these rules, and one draw needn't show every extreme that they name: `face_order`: each element's row of each face is a permutation of 0 to 124.
All inputs are finite; a program needn't handle non-finite values.
Results may differ from the reference program's by a relative error of at most 0.0049.
Values may be sent and summed in bfloat16 or wider, within the bound.
No kernel may reach another device: no remote copies, remote signals or barrier semaphores. Data moves between devices by JAX's collectives and lax.ppermute only.
A program may use at most 64 MiB of HBM per device.

```python
import jax
import jax.numpy as jnp
from jax import lax

NODE = 5
VARS = 5
ROWS = 625
TRACE = 125
RHS = 768
PLANES = 32
COLS_Y = 4
COLS_Z = 4


def draw_inverse(key, part):
    key = jax.random.fold_in(key, 11)
    noise_key, diagonal_key = jax.random.split(key)
    block_shape = (PLANES, COLS_Y, COLS_Z, ROWS, ROWS)
    off_diagonal = jnp.clip(jax.random.normal(noise_key, block_shape, jnp.float32), -3.0, 3.0) * (0.6 * ROWS ** (-0.5))
    diagonal_part = jax.random.uniform(diagonal_key, block_shape[:-1], jnp.float32, 0.5, 1.0)
    identity = (jnp.arange(ROWS)[:, None] == jnp.arange(ROWS)[None, :]).astype(jnp.float32)
    return (off_diagonal + identity * diagonal_part[..., None]).astype(jnp.bfloat16)


def draw_coupling(key, part):
    key = jax.random.fold_in(key, 23)
    block_shape = (PLANES, COLS_Y, COLS_Z, 6, ROWS, TRACE)
    side_scale = (5.0 * TRACE) ** (-0.5)
    first_scale = 0.96 * TRACE ** (-0.5)
    noise = jnp.clip(jax.random.normal(key, block_shape, jnp.float32), -3.0, 3.0)
    face_scale = jnp.where(jnp.arange(6) == 0, first_scale, side_scale).astype(jnp.float32)
    return (noise * face_scale[:, None, None]).astype(jnp.bfloat16)


def level_of(stream_key, dims, pieces, low, top_value):
    gain = 1.0
    for axis_at, parts in pieces:
        heights = jax.random.uniform(jax.random.fold_in(jax.random.fold_in(stream_key, 6), axis_at), (parts,), jnp.float32, low / len(pieces), top_value / len(pieces))
        gain = gain * jnp.repeat(jnp.exp(heights), dims[axis_at] // parts).reshape((-1,) + (1,) * (len(dims) - 1 - axis_at))
    return gain


def normal_values(own_key, extent, width, most, cuts=(), held_as=jnp.bfloat16):
    entries = jax.random.normal(own_key, extent, jnp.float32) * width
    if len(cuts) > 0:
        entries = level_of(own_key, extent, cuts, -0.22, 0.18) * entries
    return jnp.clip(entries, min=-most, max=most).astype(held_as)


def setup_inputs(seed: int = 0) -> dict:
    arg_keys = jax.random.split(jax.random.key(seed), 6)
    return {
        "right_side": normal_values(arg_keys[0], (PLANES, COLS_Y, COLS_Z, ROWS, RHS), 1.0, 6.0, ((0, 32), (1, 4), (2, 4))),
        "inverse": draw_inverse(jax.random.fold_in(arg_keys[5], 71), 0),
        "coupling": draw_coupling(jax.random.fold_in(arg_keys[5], 71), 0),
        "initial_guess": normal_values(arg_keys[3], (PLANES, COLS_Y, COLS_Z, ROWS, RHS), 1.0, 6.0, ((0, 32), (1, 4), (2, 4))),
        "face_order": jax.vmap(lambda own: jax.random.permutation(own, TRACE))(jax.random.split(arg_keys[4], PLANES * COLS_Y * COLS_Z * 6)).reshape((PLANES, COLS_Y, COLS_Z, 6, TRACE)).astype(jnp.int32),
    }


def face_trace(values, which, side):
    shaped = values.reshape(values.shape[:-2] + (VARS, NODE, NODE, NODE, values.shape[-1]))
    picked = lax.index_in_dim(shaped, side, shaped.ndim - 4 + which, keepdims=False)
    return picked.reshape(values.shape[:-2] + (VARS * NODE * NODE, values.shape[-1]))


def shift_rows(field, axis, step):
    count = field.shape[axis]
    blank = jnp.zeros_like(lax.slice_in_dim(field, 0, 1, axis=axis))
    if step > 0:
        return jnp.concatenate([blank, lax.slice_in_dim(field, 0, count - 1, axis=axis)], axis=axis)
    return jnp.concatenate([lax.slice_in_dim(field, 1, count, axis=axis), blank], axis=axis)


def reference(right_side, inverse, coupling, initial_guess, face_order):
    highest = lax.Precision.HIGHEST

    def sweep(incoming, plane_index):
        guess_here = lax.dynamic_index_in_dim(initial_guess, plane_index, 0, keepdims=False)
        next_index = jnp.minimum(plane_index + 1, PLANES - 1).astype(jnp.int32)
        guess_next = lax.dynamic_index_in_dim(initial_guess, next_index, 0, keepdims=False)
        inside = (plane_index + 1 < PLANES).astype(guess_next.dtype)
        downstream = face_trace(guess_next, 0, 0) * inside
        lower_y = shift_rows(face_trace(guess_here, 1, NODE - 1), 0, 1)
        upper_y = shift_rows(face_trace(guess_here, 1, 0), 0, -1)
        lower_z = shift_rows(face_trace(guess_here, 2, NODE - 1), 1, 1)
        upper_z = shift_rows(face_trace(guess_here, 2, 0), 1, -1)
        stacked = jnp.stack([downstream, lower_y, upper_y, lower_z, upper_z], axis=2)
        order_here = lax.dynamic_index_in_dim(face_order, plane_index, 0, keepdims=False)
        permuted = jnp.take_along_axis(stacked, order_here[:, :, 1:, :, None], axis=3)
        couple_here = lax.dynamic_index_in_dim(coupling, plane_index, 0, keepdims=False)
        pulled = jnp.einsum("yzfrt,yzftc->yzrc", couple_here[:, :, 1:].astype(jnp.float32),
                            permuted.astype(jnp.float32), precision=highest)
        rhs_here = lax.dynamic_index_in_dim(right_side, plane_index, 0, keepdims=False)
        residual_part = (rhs_here.astype(jnp.float32) - pulled).astype(jnp.bfloat16)
        inverse_here = lax.dynamic_index_in_dim(inverse, plane_index, 0, keepdims=False).astype(jnp.float32)
        solved = jnp.einsum("yzrs,yzsc->yzrc", inverse_here, residual_part.astype(jnp.float32), precision=highest)
        upstream_gain = jnp.einsum("yzrs,yzst->yzrt", inverse_here, couple_here[:, :, 0].astype(jnp.float32),
                                   precision=highest)
        arrived = jnp.take_along_axis(incoming, order_here[:, :, 0, :, None], axis=2)
        updated = solved - jnp.einsum("yzrt,yztc->yzrc", upstream_gain, arrived, precision=highest)
        return face_trace(updated, 0, NODE - 1), updated.astype(jnp.bfloat16)

    start = jnp.zeros((COLS_Y, COLS_Z, TRACE, RHS), jnp.float32)
    finish, result = lax.scan(sweep, start, jnp.arange(PLANES, dtype=jnp.int32))
    return result
```

```python
import jax
import jax.numpy as jnp
from jax import lax
from jax.experimental import pallas as pl
from jax.experimental.pallas import tpu as pltpu
from jax.sharding import PartitionSpec as P

NODE = 5
TRACE = 125
WIDE = 128
FACES = 5
GROUP = 8
f32, bf16 = jnp.float32, jnp.bfloat16
WIRE = f32
GRANT = 40 * 1024 * 1024


def params(*semantics):
    return pltpu.CompilerParams(vmem_limit_bytes=GRANT, dimension_semantics=semantics or None)


def dot(left, right, contract=(1, 0)):
    dims = (((contract[0],), (contract[1],)), ((), ()))
    return lax.dot_general(left, right, dims, preferred_element_type=f32)


def halves(value):
    high = value.astype(bf16)
    return high, (value - high.astype(f32)).astype(bf16)


def split_left(value):
    high, low = halves(value)
    return jnp.concatenate([high, low, high], axis=1)


def split_right(value, axis):
    high, low = halves(value)
    return jnp.concatenate([high, high, low], axis=axis)


def trace_rows(which, side):
    at = lax.broadcasted_iota(jnp.int32, (WIDE, 1), 0)
    var = (at * 41) >> 10
    rest = at - 25 * var
    slow = (rest * 13) >> 6
    fast = rest - 5 * slow
    place = [side, slow, fast]
    if which == 1:
        place = [slow, side, fast]
    if which == 2:
        place = [slow, fast, side]
    row = var * 125 + place[0] * 25 + place[1] * 5 + place[2]
    row = jnp.where(at < TRACE, row, -1)
    column = lax.broadcasted_iota(jnp.int32, (WIDE, 625), 1)
    return (row == column).astype(f32).astype(bf16)


SENT = ((0, 0), (1, NODE - 1), (1, 0), (2, NODE - 1), (2, 0))


def traces_kernel(guess, *outs):
    for (which, side), out in zip(SENT, outs):
        out[...] = dot(trace_rows(which, side), guess[...]).astype(bf16)


def maps_kernel(inverse, coupling, order, couple_out, gain_out, inverse_out, map_out):
    node = lax.broadcasted_iota(jnp.int32, (WIDE, TRACE), 0)

    def permuted(face):
        pick = (node == order[face : face + 1, :]).astype(f32).astype(bf16)
        return dot(coupling[face], pick, (1, 1)).astype(bf16)

    for face in range(1, 6):
        couple_out[:, (face - 1) * WIDE : face * WIDE] = permuted(face)
    first = permuted(0)
    gain_out[...] = split_left(dot(inverse[...], first))
    picked = dot(trace_rows(0, NODE - 1), inverse[...]).astype(bf16)
    inverse_out[...] = picked
    map_out[...] = -dot(picked, first).T


def offset_kernel(right_side, couple, t1, t2, t3, t4, t5, inverse, maps, residual_out, send_out):
    traces = jnp.concatenate([t[...] for t in (t1, t2, t3, t4, t5)], axis=0)
    pulled = dot(couple[...], traces)
    residual = (right_side[...].astype(f32) - pulled).astype(bf16)
    residual_out[...] = residual
    offset = dot(inverse[...], residual).T
    part = send_out.shape[1] - WIDE
    for at in range(send_out.shape[0]):
        send_out[at, :part, :] = offset[at * part : (at + 1) * part].astype(WIRE)
        send_out[at, part:, :] = maps[...].astype(WIRE)


def scan_kernel(received, states_out, last_out):
    count, rows, _ = received.shape
    part = rows - WIDE
    state = received[0].astype(f32)
    for at in range(1, count):
        states_out[at - 1] = state
        step = received[at].astype(f32)
        moved = dot(split_left(state), split_right(step[part:], 0))
        state = jnp.concatenate([moved[:part] + step[:part], moved[part:]], axis=0)
    last_out[...] = state.astype(WIRE)


def prefix_kernel(group, totals, states, out):
    count, part, _ = out.shape
    entering = jnp.zeros((part, WIDE), f32)
    for at in range(totals.shape[0] - 1):
        total = totals[at].astype(f32)
        longer = total[:part]
        if at > 0:
            longer = longer + dot(split_left(entering), split_right(total[part:], 0))
        entering = jnp.where(at < group[0], longer, entering)
    out[0] = entering.astype(WIRE)
    left = split_left(entering)
    for at in range(1, count):
        state = states[at - 1]
        moved = dot(left, split_right(state[part:], 0))
        out[at] = (state[:part] + moved).astype(WIRE)


def update_kernel(inverse, residual, gain, arrived, out):
    solved = dot(inverse[...], residual[...])
    moved = dot(gain[...], split_right(arrived[...].astype(f32), 1), (1, 1))
    out[...] = (solved - moved).astype(bf16)


def on_device(right_side, inverse, coupling, initial_guess, face_order):
    rows, width = right_side.shape[-2:]
    right_side, inverse, guess = right_side[0, 0, 0], inverse[0, 0, 0], initial_guess[0, 0, 0]
    coupling, order = coupling[0, 0, 0], face_order[0, 0, 0]
    count = lax.axis_size("stream")
    groups = count // GROUP
    part = width // GROUP
    near = [[g * GROUP + i for i in range(GROUP)] for g in range(groups)]
    far = [[g * GROUP + i for g in range(groups)] for i in range(GROUP)]

    def whole(*shape):
        return pl.BlockSpec(shape, lambda *_: (0,) * len(shape))

    def columns(size, block):
        return pl.BlockSpec((size, block), lambda i: (0, i))

    traces = pl.pallas_call(
        traces_kernel,
        grid=(3,),
        in_specs=[columns(rows, width // 3)],
        out_specs=[columns(WIDE, width // 3)] * FACES,
        out_shape=[jax.ShapeDtypeStruct((WIDE, width), bf16)] * FACES,
        compiler_params=params("arbitrary"),
        name="face_traces",
    )(guess)

    def shifted(value, axis, step):
        size = lax.axis_size(axis)
        pairs = [(i, i + step) for i in range(size) if 0 <= i + step < size]
        return lax.ppermute(value, axis, pairs)

    moves = (("stream", -1), ("gy", 1), ("gy", -1), ("gz", 1), ("gz", -1))
    halos = [shifted(value, axis, step) for value, (axis, step) in zip(traces, moves)]

    couple, gain, picked, maps = pl.pallas_call(
        maps_kernel,
        out_shape=[
            jax.ShapeDtypeStruct((rows, FACES * WIDE), bf16),
            jax.ShapeDtypeStruct((rows, 3 * WIDE), bf16),
            jax.ShapeDtypeStruct((WIDE, rows), bf16),
            jax.ShapeDtypeStruct((WIDE, WIDE), f32),
        ],
        compiler_params=params(),
        name="element_maps",
    )(inverse, coupling, order)

    block = width // 2
    residual, sent = pl.pallas_call(
        offset_kernel,
        grid=(2,),
        in_specs=[columns(rows, block), whole(rows, FACES * WIDE)]
        + [columns(WIDE, block)] * FACES
        + [whole(WIDE, rows), whole(WIDE, WIDE)],
        out_specs=[
            columns(rows, block),
            pl.BlockSpec((GROUP // 2, part + WIDE, WIDE), lambda i: (i, 0, 0)),
        ],
        out_shape=[
            jax.ShapeDtypeStruct((rows, width), bf16),
            jax.ShapeDtypeStruct((GROUP, part + WIDE, WIDE), WIRE),
        ],
        compiler_params=params("arbitrary"),
        name="residual_offset",
    )(right_side, couple, *halos, picked, maps)

    received = lax.all_to_all(sent, "stream", 0, 0, tiled=True, axis_index_groups=near)
    states, last = pl.pallas_call(
        scan_kernel,
        out_shape=[
            jax.ShapeDtypeStruct((GROUP - 1, part + WIDE, WIDE), f32),
            jax.ShapeDtypeStruct((part + WIDE, WIDE), WIRE),
        ],
        compiler_params=params(),
        name="group_scan",
    )(received)

    totals = lax.all_gather(last, "stream", axis_index_groups=far)
    group = (lax.axis_index("stream") // GROUP).astype(jnp.int32).reshape(1)
    entering = pl.pallas_call(
        prefix_kernel,
        in_specs=[
            pl.BlockSpec(memory_space=pltpu.SMEM),
            pl.BlockSpec(memory_space=pltpu.VMEM),
            pl.BlockSpec(memory_space=pltpu.VMEM),
        ],
        out_shape=jax.ShapeDtypeStruct((GROUP, part, WIDE), WIRE),
        compiler_params=params(),
        name="group_prefix",
    )(group, totals, states)
    arrived = lax.all_to_all(entering, "stream", 0, 0, tiled=True, axis_index_groups=near)

    updated = pl.pallas_call(
        update_kernel,
        grid=(3,),
        in_specs=[
            whole(rows, rows),
            columns(rows, width // 3),
            whole(rows, 3 * WIDE),
            pl.BlockSpec((width // 3, WIDE), lambda i: (i, 0)),
        ],
        out_specs=columns(rows, width // 3),
        out_shape=jax.ShapeDtypeStruct((rows, width), bf16),
        compiler_params=params("arbitrary"),
        name="update",
    )(inverse, residual, gain, arrived.reshape(width, WIDE))
    return updated[None, None, None]


def solution(mesh):
    return jax.shard_map(
        on_device,
        mesh=mesh,
        in_specs=(
            P("stream", "gy", "gz", None, None),
            P("stream", "gy", "gz", None, None),
            P("stream", "gy", "gz", None, None, None),
            P("stream", "gy", "gz", None, None),
            P("stream", "gy", "gz", None, None),
        ),
        out_specs=P("stream", "gy", "gz", None, None),
        check_vma=False,
    )
```

```python
import jax
import jax.numpy as jnp
from jax import lax
from jax.experimental import pallas as pl
from jax.experimental.pallas import tpu as pltpu
from jax.sharding import PartitionSpec as P

NODE = 5
TRACE = 125
WIDE = 128
FACES = 5
GROUP = 8
f32, bf16 = jnp.float32, jnp.bfloat16
WIRE = jnp.int16
GRANT = 40 * 1024 * 1024


def params():
    return pltpu.CompilerParams(vmem_limit_bytes=GRANT)


def dot(left, right, contract=(1, 0)):
    dims = (((contract[0],), (contract[1],)), ((), ()))
    return lax.dot_general(left, right, dims, preferred_element_type=f32)


def halves(value):
    high = value.astype(bf16)
    return high, (value - high.astype(f32)).astype(bf16)


def split_left(value):
    high, low = halves(value)
    return jnp.concatenate([high, low, high], axis=1)


def split_right(value, axis):
    high, low = halves(value)
    return jnp.concatenate([high, high, low], axis=axis)


def coded(value):
    lane = lax.broadcasted_iota(jnp.int32, value.shape, 1)
    top = jnp.max(jnp.abs(value), axis=1, keepdims=True)
    power = jnp.minimum(jnp.ceil(jnp.log2(jnp.maximum(top, 1e-30))), 127.0)
    fraction = jnp.round(value * jnp.exp2(13.9 - power))
    return jnp.where(lane == WIDE - 1, power, fraction).astype(jnp.int32).astype(WIRE)


def decoded(block):
    value = block.astype(jnp.int32).astype(f32)
    lane = lax.broadcasted_iota(jnp.int32, value.shape, 1)
    power = value[:, WIDE - 1 :]
    return jnp.where(lane == WIDE - 1, 0.0, value * jnp.exp2(power - 13.9))


def trace_rows(which, side):
    at = lax.broadcasted_iota(jnp.int32, (WIDE, 1), 0)
    var = (at * 41) >> 10
    rest = at - 25 * var
    slow = (rest * 13) >> 6
    fast = rest - 5 * slow
    place = [side, slow, fast]
    if which == 1:
        place = [slow, side, fast]
    if which == 2:
        place = [slow, fast, side]
    row = var * 125 + place[0] * 25 + place[1] * 5 + place[2]
    row = jnp.where(at < TRACE, row, -1)
    column = lax.broadcasted_iota(jnp.int32, (WIDE, 625), 1)
    return (row == column).astype(f32).astype(bf16)


SENT = ((0, 0), (1, NODE - 1), (1, 0), (2, NODE - 1), (2, 0))


def traces_kernel(guess, *refs):
    outs, (held, sems) = refs[:FACES], refs[FACES:]
    block = WIDE * 2
    cuts = [slice(at, at + block) for at in range(0, held.shape[1], block)]
    copies = [
        pltpu.make_async_copy(guess.at[:, cut], held.at[:, cut], sems.at[at])
        for at, cut in enumerate(cuts)
    ]
    for copy in copies:
        copy.start()
    picks = [trace_rows(which, side) for which, side in SENT]
    for copy, cut in zip(copies, cuts):
        copy.wait()
        for pick, out in zip(picks, outs):
            out[:, cut] = dot(pick, held[:, cut]).astype(bf16)


def maps_kernel(inverse, coupling, order, couple_out, gain_out, inverse_out, map_out):
    node = lax.broadcasted_iota(jnp.int32, (WIDE, TRACE), 0)

    def permuted(face):
        pick = (node == order[face : face + 1, :]).astype(f32).astype(bf16)
        return dot(coupling[face], pick, (1, 1)).astype(bf16)

    for face in range(1, 6):
        couple_out[:, (face - 1) * WIDE : face * WIDE] = permuted(face)
    first = permuted(0)
    gain_out[...] = split_left(dot(inverse[...], first))
    picked = dot(trace_rows(0, NODE - 1), inverse[...]).astype(bf16)
    inverse_out[...] = picked
    map_out[...] = -dot(picked, first).T


def offset_kernel(right_side, couple, t1, t2, t3, t4, t5, inverse, maps, residual_out, send_out):
    count, rows, _ = send_out.shape
    part = rows - WIDE
    step = coded(maps[...])
    for start in range(0, count, count // 2):
        cut = slice(start * part, (start + count // 2) * part)
        traces = jnp.concatenate([t[:, cut] for t in (t1, t2, t3, t4, t5)], axis=0)
        pulled = dot(couple[...], traces)
        residual = (right_side[:, cut].astype(f32) - pulled).astype(bf16)
        residual_out[:, cut] = residual
        offset = coded(dot(inverse[...], residual).T)
        for at in range(count // 2):
            send_out[start + at, :part, :] = offset[at * part : (at + 1) * part]
            send_out[start + at, part:, :] = step


def scan_kernel(received, states_out, total_out):
    count, rows, _ = received.shape
    part = rows - WIDE
    state = decoded(received[0])
    for at in range(1, count):
        states_out[at - 1] = state
        step = decoded(received[at])
        moved = dot(split_left(state), split_right(step[part:], 0))
        state = jnp.concatenate([moved[:part] + step[:part], moved[part:]], axis=0)
    states_out[count - 1] = state
    total_out[...] = coded(state[:part])


def passing_kernel(entering, last, out):
    part = out.shape[0]
    moved = dot(split_left(decoded(entering[...])), split_right(last[0, part:], 0))
    out[...] = coded(last[0, :part] + moved)


def prefix_kernel(*refs):
    entries, states, out = refs[:-2], refs[-2], refs[-1]
    count, part, _ = out.shape
    entering = sum(decoded(entry[...]) for entry in entries)
    out[0] = coded(entering)
    left = split_left(entering)
    for at in range(1, count):
        state = states[at - 1]
        moved = dot(left, split_right(state[part:], 0))
        out[at] = coded(state[:part] + moved)


def update_kernel(inverse, residual, gain, arrived, out, held, sems):
    block = WIDE * 2
    copies = []
    for at, start in enumerate(range(0, held.shape[1], block)):
        cut = slice(start, start + block)
        moved = dot(gain[...], split_right(decoded(arrived[cut, :]), 1), (1, 1))
        held[:, cut] = (dot(inverse[...], residual[:, cut]) - moved).astype(bf16)
        copies.append(pltpu.make_async_copy(held.at[:, cut], out.at[:, cut], sems.at[at]))
        copies[-1].start()
    for copy in copies:
        copy.wait()


def on_device(right_side, inverse, coupling, initial_guess, face_order):
    rows, width = right_side.shape[-2:]
    right_side, inverse, guess = right_side[0, 0, 0], inverse[0, 0, 0], initial_guess[0, 0, 0]
    coupling, order = coupling[0, 0, 0], face_order[0, 0, 0]
    count = lax.axis_size("stream")
    groups = count // GROUP
    part = width // GROUP
    near = [[g * GROUP + i for i in range(GROUP)] for g in range(groups)]

    outer = pl.BlockSpec(memory_space=pltpu.HBM)
    blocks = width // (2 * WIDE)

    traces = pl.pallas_call(
        traces_kernel,
        in_specs=[outer],
        out_shape=[jax.ShapeDtypeStruct((WIDE, width), bf16)] * FACES,
        scratch_shapes=[pltpu.VMEM((rows, width), bf16), pltpu.SemaphoreType.DMA((blocks,))],
        compiler_params=params(),
        name="face_traces",
    )(guess)

    def shifted(value, axis, step):
        size = lax.axis_size(axis)
        pairs = [(i, i + step) for i in range(size) if 0 <= i + step < size]
        return lax.ppermute(value, axis, pairs)

    moves = (("stream", -1), ("gy", 1), ("gy", -1), ("gz", 1), ("gz", -1))
    halos = [shifted(value, axis, step) for value, (axis, step) in zip(traces, moves)]

    couple, gain, picked, maps = pl.pallas_call(
        maps_kernel,
        out_shape=[
            jax.ShapeDtypeStruct((rows, FACES * WIDE), bf16),
            jax.ShapeDtypeStruct((rows, 3 * WIDE), bf16),
            jax.ShapeDtypeStruct((WIDE, rows), bf16),
            jax.ShapeDtypeStruct((WIDE, WIDE), f32),
        ],
        compiler_params=params(),
        name="element_maps",
    )(inverse, coupling, order)

    residual, sent = pl.pallas_call(
        offset_kernel,
        out_shape=[
            jax.ShapeDtypeStruct((rows, width), bf16),
            jax.ShapeDtypeStruct((GROUP, part + WIDE, WIDE), WIRE),
        ],
        compiler_params=params(),
        name="residual_offset",
    )(right_side, couple, *halos, picked, maps)

    received = lax.all_to_all(sent, "stream", 0, 0, tiled=True, axis_index_groups=near)
    states, total = pl.pallas_call(
        scan_kernel,
        out_shape=[
            jax.ShapeDtypeStruct((GROUP, part + WIDE, WIDE), f32),
            jax.ShapeDtypeStruct((part, WIDE), WIRE),
        ],
        compiler_params=params(),
        name="group_scan",
    )(received)

    entries = []
    for g in range(groups - 1):
        pairs = [(g * GROUP + i, (g + 1) * GROUP + i) for i in range(GROUP)]
        entries.append(lax.ppermute(total, "stream", pairs))
        if g < groups - 2:
            total = pl.pallas_call(
                passing_kernel,
                grid=(1,),
                in_specs=[
                    pl.BlockSpec((part, WIDE), lambda i: (0, 0)),
                    pl.BlockSpec((1, part + WIDE, WIDE), lambda i: (GROUP - 1, 0, 0)),
                ],
                out_specs=pl.BlockSpec((part, WIDE), lambda i: (0, 0)),
                out_shape=jax.ShapeDtypeStruct((part, WIDE), WIRE),
                compiler_params=params(),
                name="group_total",
            )(entries[-1], states)
    entering = pl.pallas_call(
        prefix_kernel,
        out_shape=jax.ShapeDtypeStruct((GROUP, part, WIDE), WIRE),
        compiler_params=params(),
        name="group_prefix",
    )(*entries, states)
    arrived = lax.all_to_all(entering, "stream", 0, 0, tiled=True, axis_index_groups=near)

    updated = pl.pallas_call(
        update_kernel,
        out_specs=outer,
        out_shape=jax.ShapeDtypeStruct((rows, width), bf16),
        scratch_shapes=[pltpu.VMEM((rows, width), bf16), pltpu.SemaphoreType.DMA((blocks,))],
        compiler_params=params(),
        name="update",
    )(inverse, residual, gain, arrived.reshape(width, WIDE))
    return updated[None, None, None]


def solution(mesh):
    return jax.shard_map(
        on_device,
        mesh=mesh,
        in_specs=(
            P("stream", "gy", "gz", None, None),
            P("stream", "gy", "gz", None, None),
            P("stream", "gy", "gz", None, None, None),
            P("stream", "gy", "gz", None, None),
            P("stream", "gy", "gz", None, None),
        ),
        out_specs=P("stream", "gy", "gz", None, None),
        check_vma=False,
    )
```

```python
import jax
import jax.numpy as jnp
from jax import lax
from jax.experimental import pallas as pl
from jax.experimental.pallas import tpu as pltpu
from jax.sharding import PartitionSpec as P

NODE = 5
TRACE = 125
WIDE = 128
TALL = 640
FACES = 5
GROUP = 8
f32, bf16 = jnp.float32, jnp.bfloat16
WIRE = jnp.int16
GRANT = 40 * 1024 * 1024


def params():
    return pltpu.CompilerParams(vmem_limit_bytes=GRANT)


def dot(left, right, contract=(1, 0)):
    dims = (((contract[0],), (contract[1],)), ((), ()))
    return lax.dot_general(left, right, dims, preferred_element_type=f32)


def halves(value):
    high = value.astype(bf16)
    return high, (value - high.astype(f32)).astype(bf16)


def split_left(value):
    high, low = halves(value)
    return jnp.concatenate([high, low, high], axis=1)


def split_right(value, axis):
    high, low = halves(value)
    return jnp.concatenate([high, high, low], axis=axis)


def coded(value):
    lane = lax.broadcasted_iota(jnp.int32, value.shape, 1)
    top = jnp.max(jnp.abs(value), axis=1, keepdims=True)
    power = jnp.minimum(jnp.ceil(jnp.log2(jnp.maximum(top, 1e-30))), 127.0)
    fraction = jnp.round(value * jnp.exp2(13.9 - power))
    return jnp.where(lane == WIDE - 1, power, fraction).astype(jnp.int32).astype(WIRE)


def decoded(block):
    value = block.astype(jnp.int32).astype(f32)
    lane = lax.broadcasted_iota(jnp.int32, value.shape, 1)
    power = value[:, WIDE - 1 :]
    return jnp.where(lane == WIDE - 1, 0.0, value * jnp.exp2(power - 13.9))


def trace_rows(which, side):
    at = lax.broadcasted_iota(jnp.int32, (WIDE, 1), 0)
    var = (at * 41) >> 10
    rest = at - 25 * var
    slow = (rest * 13) >> 6
    fast = rest - 5 * slow
    place = [side, slow, fast]
    if which == 1:
        place = [slow, side, fast]
    if which == 2:
        place = [slow, fast, side]
    row = var * 125 + place[0] * 25 + place[1] * 5 + place[2]
    row = jnp.where(at < TRACE, row, -1)
    column = lax.broadcasted_iota(jnp.int32, (WIDE, 625), 1)
    return (row == column).astype(f32).astype(bf16)


def traces_kernel(core, guess, *outs):
    last = NODE - 1
    ahead = last * (1 - core[0])
    sent = ((0, 0), (1, ahead), (2, ahead), (1, last - ahead), (2, last - ahead))
    for (which, side), out in zip(sent, outs):
        out[...] = dot(trace_rows(which, side), guess[...]).astype(bf16)


def maps_kernel(core, inverse, coupling, order, couple_out, left_out, inverse_out, map_out):
    node = lax.broadcasted_iota(jnp.int32, (WIDE, TRACE), 0)

    def permuted(face):
        pick = (node == order[face]).astype(f32).astype(bf16)
        return dot(coupling[face], pick, (1, 1)).astype(bf16)

    turn = core[0]
    for at, face in enumerate((1, 2 + turn, 4 + turn, 3 - turn, 5 - turn)):
        couple_out[:, at * WIDE : (at + 1) * WIDE] = permuted(face)
    first = permuted(0)
    left_out[...] = jnp.zeros(left_out.shape, bf16)
    left_out[:, : inverse.shape[1]] = inverse[...]
    left_out[:, TALL:] = split_left(-dot(inverse[...], first))
    picked = dot(trace_rows(0, NODE - 1), inverse[...]).astype(bf16)
    inverse_out[...] = picked
    map_out[...] = -dot(picked, first).T


def partial_kernel(right_side, couple, t1, t2, t3, t4, out):
    traces = jnp.concatenate([t[...] for t in (t1, t2, t3, t4)], axis=0)
    out[...] = right_side[...].astype(f32) - dot(couple[:, : 4 * WIDE], traces)


def offset_kernel(partial, couple, t5, inverse, maps, residual_out, send_out):
    count, rows, _ = send_out.shape
    part = rows - WIDE
    step = coded(maps[...])
    for start in range(0, count, count // 2):
        cut = slice(start * part, (start + count // 2) * part)
        pulled = dot(couple[:, 4 * WIDE :], t5[:, cut])
        residual = (partial[:, cut] - pulled).astype(bf16)
        padding = jnp.zeros((residual_out.shape[0] - residual.shape[0], residual.shape[1]), bf16)
        residual_out[:, cut] = jnp.concatenate([residual, padding], axis=0)
        offset = coded(dot(inverse[...], residual).T)
        for at in range(count // 2):
            send_out[start + at, :part, :] = offset[at * part : (at + 1) * part]
            send_out[start + at, part:, :] = step


def scan_kernel(received, states_out, total_out, both_out):
    count, rows, _ = received.shape
    part = rows - WIDE
    state = decoded(received[0])
    for at in range(1, count):
        states_out[at - 1] = state
        step = decoded(received[at])
        moved = dot(split_left(state), split_right(step[part:], 0))
        state = jnp.concatenate([moved[:part] + step[:part], moved[part:]], axis=0)
    whole = coded(state)
    total_out[...] = whole[:part]
    both_out[...] = whole


def passed(entering, state):
    part = entering.shape[0]
    return state[:part] + dot(split_left(entering), split_right(state[part:], 0))


def pair_kernel(group, own, above, below, out):
    part = out.shape[0]
    first = group[0] == 0
    mine = decoded(own[...])
    state = jnp.where(first, decoded(above[...]), mine)
    entering = jnp.where(first, mine[:part], decoded(below[...]))
    out[...] = coded(passed(entering, state))


def prefix_kernel(group, first, pair, third, states, out):
    count, part, _ = out.shape
    entering = decoded(pair[...])
    later = passed(entering, decoded(third[...]))
    entering = jnp.where(group[0] == 3, later, entering) + decoded(first[...])
    out[0] = coded(entering)
    left = split_left(entering)
    for at in range(1, count):
        state = states[at - 1]
        moved = dot(left, split_right(state[part:], 0))
        out[at] = coded(state[:part] + moved)


def update_kernel(left, residual, arrived, out, held, sems):
    block = WIDE * 2
    copies = []
    for at, start in enumerate(range(0, held.shape[1], block)):
        cut = slice(start, start + block)
        entering = split_right(decoded(arrived[cut, :]).T, 0)
        right = jnp.concatenate([residual[:, cut], entering], axis=0)
        held[:, cut] = dot(left[...], right).astype(bf16)
        copies.append(pltpu.make_async_copy(held.at[:, cut], out.at[:, cut], sems.at[at]))
        copies[-1].start()
    for copy in copies:
        copy.wait()


def on_device(right_side, inverse, coupling, initial_guess, face_order):
    rows, width = right_side.shape[-2:]
    right_side, inverse, guess = right_side[0, 0, 0], inverse[0, 0, 0], initial_guess[0, 0, 0]
    coupling, order = coupling[0, 0, 0], face_order[0, 0, 0]
    count = lax.axis_size("stream")
    assert count == 4 * GROUP
    part = width // GROUP
    near = [[g * GROUP + i for i in range(GROUP)] for g in range(4)]

    outer = pl.BlockSpec(memory_space=pltpu.HBM)
    blocks = width // (2 * WIDE)

    scalar = pl.BlockSpec(memory_space=pltpu.SMEM)
    inner = pl.BlockSpec(memory_space=pltpu.VMEM)
    place = lax.axis_index("stream").astype(jnp.int32)
    core, group = (place & 1).reshape(1), (place >> 3).reshape(1)
    assert GROUP == 8 and lax.axis_size("gy") == lax.axis_size("gz")

    traces = pl.pallas_call(
        traces_kernel,
        in_specs=[scalar, inner],
        out_shape=[jax.ShapeDtypeStruct((WIDE, width), bf16)] * FACES,
        compiler_params=params(),
        cost_estimate=pl.CostEstimate(flops=8 * 10**9, bytes_accessed=2 * rows * width, transcendentals=0),
        name="face_traces",
    )(core, guess)

    size = lax.axis_size("gy")

    def upstream(value):
        return lax.ppermute(value, "stream", [(i, i - 1) for i in range(1, count)])

    def sideways(value, axis, first):
        steps = [first if i % 2 == 0 else -first for i in range(count)]
        pairs = [
            (i * size + j, i * size + j + steps[i])
            for i in range(count)
            for j in range(size)
            if 0 <= j + steps[i] < size
        ]
        return lax.ppermute(value, ("stream", axis), pairs)

    halos = [upstream(traces[0])]
    for at, (axis, first) in enumerate((("gy", 1), ("gz", 1), ("gy", -1), ("gz", -1))):
        halos.append(sideways(traces[1 + at], axis, first))

    couple, left, picked, maps = pl.pallas_call(
        maps_kernel,
        in_specs=[scalar, inner, inner, inner],
        out_shape=[
            jax.ShapeDtypeStruct((rows, FACES * WIDE), bf16),
            jax.ShapeDtypeStruct((rows, TALL + 3 * WIDE), bf16),
            jax.ShapeDtypeStruct((WIDE, rows), bf16),
            jax.ShapeDtypeStruct((WIDE, WIDE), f32),
        ],
        compiler_params=params(),
        name="element_maps",
    )(core, inverse, coupling, order.reshape(6, 1, TRACE))

    partial = pl.pallas_call(
        partial_kernel,
        out_shape=jax.ShapeDtypeStruct((rows, width), f32),
        cost_estimate=pl.CostEstimate(
            flops=8 * WIDE * rows * width, bytes_accessed=6 * rows * width, transcendentals=0
        ),
        compiler_params=params(),
        name="partial_residual",
    )(right_side, couple, *halos[:4])
    residual, sent = pl.pallas_call(
        offset_kernel,
        out_shape=[
            jax.ShapeDtypeStruct((TALL, width), bf16),
            jax.ShapeDtypeStruct((GROUP, part + WIDE, WIDE), WIRE),
        ],
        compiler_params=params(),
        name="residual_offset",
    )(partial, couple, halos[4], picked, maps)

    received = lax.all_to_all(sent, "stream", 0, 0, tiled=True, axis_index_groups=near)
    states, total, both = pl.pallas_call(
        scan_kernel,
        out_shape=[
            jax.ShapeDtypeStruct((GROUP - 1, part + WIDE, WIDE), f32),
            jax.ShapeDtypeStruct((part, WIDE), WIRE),
            jax.ShapeDtypeStruct((part + WIDE, WIDE), WIRE),
        ],
        compiler_params=params(),
        name="group_scan",
    )(received)

    def between(value, *pairs):
        moves = [(a * GROUP + i, b * GROUP + i) for a, b in pairs for i in range(GROUP)]
        return lax.ppermute(value, "stream", moves)

    above = between(both, (1, 0))
    first = between(total, (0, 1))
    third = between(both, (2, 3))
    pair = pl.pallas_call(
        pair_kernel,
        in_specs=[scalar] + [inner] * 3,
        out_shape=jax.ShapeDtypeStruct((part, WIDE), WIRE),
        compiler_params=params(),
        name="pair_total",
    )(group, both, above, first)
    pair = between(pair, (1, 2), (0, 3))
    entering = pl.pallas_call(
        prefix_kernel,
        in_specs=[scalar] + [inner] * 4,
        out_shape=jax.ShapeDtypeStruct((GROUP, part, WIDE), WIRE),
        compiler_params=params(),
        name="group_prefix",
    )(group, first, pair, third, states)
    arrived = lax.all_to_all(entering, "stream", 0, 0, tiled=True, axis_index_groups=near)

    updated = pl.pallas_call(
        update_kernel,
        out_specs=outer,
        out_shape=jax.ShapeDtypeStruct((rows, width), bf16),
        scratch_shapes=[pltpu.VMEM((rows, width), bf16), pltpu.SemaphoreType.DMA((blocks,))],
        compiler_params=params(),
        name="update",
    )(left, residual, arrived.reshape(width, WIDE))
    return updated[None, None, None]


def solution(mesh):
    return jax.shard_map(
        on_device,
        mesh=mesh,
        in_specs=(
            P("stream", "gy", "gz", None, None),
            P("stream", "gy", "gz", None, None),
            P("stream", "gy", "gz", None, None, None),
            P("stream", "gy", "gz", None, None),
            P("stream", "gy", "gz", None, None),
        ),
        out_specs=P("stream", "gy", "gz", None, None),
        check_vma=False,
    )
```

```python
import jax
import jax.numpy as jnp
from jax import lax
from jax.experimental import pallas as pl
from jax.experimental.pallas import tpu as pltpu
from jax.sharding import PartitionSpec as P

NODE = 5
TRACE = 125
WIDE = 128
TALL = 640
FACES = 5
GROUP = 8
f32, bf16 = jnp.float32, jnp.bfloat16
WIRE = jnp.int16
GRANT = 40 * 1024 * 1024


def params():
    return pltpu.CompilerParams(vmem_limit_bytes=GRANT)


def dot(left, right, contract=(1, 0)):
    dims = (((contract[0],), (contract[1],)), ((), ()))
    return lax.dot_general(left, right, dims, preferred_element_type=f32)


def halves(value):
    high = value.astype(bf16)
    return high, (value - high.astype(f32)).astype(bf16)


def split_left(value):
    high, low = halves(value)
    return jnp.concatenate([high, low, high], axis=1)


def split_right(value, axis):
    high, low = halves(value)
    return jnp.concatenate([high, high, low], axis=axis)


def coded(value):
    lane = lax.broadcasted_iota(jnp.int32, value.shape, 1)
    top = jnp.max(jnp.abs(value), axis=1, keepdims=True)
    power = jnp.minimum(jnp.ceil(jnp.log2(jnp.maximum(top, 1e-30))), 127.0)
    fraction = jnp.round(value * jnp.exp2(13.9 - power))
    return jnp.where(lane == WIDE - 1, power, fraction).astype(jnp.int32).astype(WIRE)


def decoded(block):
    value = block.astype(jnp.int32).astype(f32)
    lane = lax.broadcasted_iota(jnp.int32, value.shape, 1)
    power = value[:, WIDE - 1 :]
    return jnp.where(lane == WIDE - 1, 0.0, value * jnp.exp2(power - 13.9))


def trace_rows(which, side):
    at = lax.broadcasted_iota(jnp.int32, (WIDE, 1), 0)
    var = (at * 41) >> 10
    rest = at - 25 * var
    slow = (rest * 13) >> 6
    fast = rest - 5 * slow
    place = [side, slow, fast]
    if which == 1:
        place = [slow, side, fast]
    if which == 2:
        place = [slow, fast, side]
    row = var * 125 + place[0] * 25 + place[1] * 5 + place[2]
    row = jnp.where(at < TRACE, row, -1)
    column = lax.broadcasted_iota(jnp.int32, (WIDE, 625), 1)
    return (row == column).astype(f32).astype(bf16)


def traces_kernel(core, guess, *outs):
    last = NODE - 1
    y, z = last * (1 - core[0]), last * (core[0])
    sent = ((0, 0), (1, y), (2, z), (1, last - y), (2, last - z))
    for (which, side), out in zip(sent, outs):
        out[...] = dot(trace_rows(which, side), guess[...]).astype(bf16)


def maps_kernel(core, inverse, coupling, order, couple_out, left_out, inverse_out, map_out):
    node = lax.broadcasted_iota(jnp.int32, (WIDE, TRACE), 0)

    def permuted(face):
        pick = (node == order[face]).astype(f32).astype(bf16)
        return dot(coupling[face], pick, (1, 1)).astype(bf16)

    turn = core[0]
    for at, face in enumerate((2 + turn, 5 - turn, 1, 3 - turn, 4 + turn)):
        couple_out[:, at * WIDE : (at + 1) * WIDE] = permuted(face)
    first = permuted(0)
    left_out[...] = jnp.zeros(left_out.shape, bf16)
    left_out[:, : inverse.shape[1]] = inverse[...]
    left_out[:, TALL:] = split_left(-dot(inverse[...], first))
    picked = dot(trace_rows(0, NODE - 1), inverse[...]).astype(bf16)
    inverse_out[...] = picked
    map_out[...] = coded(-dot(picked, first).T)


def partial_kernel(right_side, couple, t1, t2, t3, t4, out):
    traces = jnp.concatenate([t[...] for t in (t1, t2, t3, t4)], axis=0)
    out[...] = right_side[...].astype(f32) - dot(couple[:, : 4 * WIDE], traces)


def offset_kernel(partial, couple, t5, inverse, residual_out, offset_out):
    block = offset_out.shape[0] // 2
    for start in (0, block):
        cut = slice(start, start + block)
        pulled = dot(couple[:, 4 * WIDE :], t5[:, cut])
        residual = (partial[:, cut] - pulled).astype(bf16)
        padding = jnp.zeros((residual_out.shape[0] - residual.shape[0], block), bf16)
        residual_out[:, cut] = jnp.concatenate([residual, padding], axis=0)
        offset_out[cut, :] = coded(dot(inverse[...], residual).T)


def merge_kernel(core, offsets, maps, send_out):
    count, rows, _ = send_out.shape
    half = rows - WIDE // 2
    last = split_right(decoded(maps[1]), 0)
    merged = decoded(offsets[1]) + dot(split_left(decoded(offsets[0])), last)
    step = dot(split_left(decoded(maps[0])), last)
    first = core[0] == 0
    step = coded(jnp.where(first, step[: WIDE // 2], step[WIDE // 2 :]))
    for at in range(count):
        low = merged[2 * at * half : (2 * at + 1) * half]
        high = merged[(2 * at + 1) * half : (2 * at + 2) * half]
        send_out[at, :half, :] = coded(jnp.where(first, low, high))
        send_out[at, half:, :] = step


def scan_kernel(received, states_out, total_out, both_out):
    count, rows, _ = received.shape
    half = rows - WIDE // 2
    part = 2 * half
    steps = []
    for at in range(0, count, 2):
        low, high = decoded(received[at]), decoded(received[at + 1])
        steps.append((low[:half], high[:half], low[half:], high[half:]))
    state = jnp.concatenate(steps[0], axis=0)
    for at in range(1, count // 2):
        states_out[at - 1] = state
        moved = dot(split_left(state), split_right(jnp.concatenate(steps[at][2:], axis=0), 0))
        offset = jnp.concatenate(steps[at][:2], axis=0)
        state = jnp.concatenate([moved[:part] + offset, moved[part:]], axis=0)
    whole = coded(state)
    total_out[...] = whole[:part]
    both_out[...] = whole


def passed(entering, state):
    part = entering.shape[0]
    return state[:part] + dot(split_left(entering), split_right(state[part:], 0))


def pair_kernel(group, own, above, below, out):
    part = out.shape[0]
    first = group[0] == 0
    mine = decoded(own[...])
    state = jnp.where(first, decoded(above[...]), mine)
    entering = jnp.where(first, mine[:part], decoded(below[...]))
    out[...] = coded(passed(entering, state))


def prefix_kernel(group, first, pair, third, states, out):
    count, part, _ = out.shape
    entering = decoded(pair[...])
    later = passed(entering, decoded(third[...]))
    entering = jnp.where(group[0] == 3, later, entering) + decoded(first[...])
    left = split_left(entering)
    for at in range(0, count, 2):
        value = entering
        if at > 0:
            state = states[at // 2 - 1]
            value = state[:part] + dot(left, split_right(state[part:], 0))
        value = coded(value)
        out[at] = value
        out[at + 1] = value


def update_kernel(core, left, residual, arrived, offsets, maps, out, held, sems):
    block = WIDE * 2
    copies = []
    step = split_right(decoded(maps[0]), 0)
    for at, start in enumerate(range(0, held.shape[1], block)):
        cut = slice(start, start + block)
        entering = decoded(arrived[cut, :])
        later = decoded(offsets[0, cut, :]) + dot(split_left(entering), step)
        entering = jnp.where(core[0] == 0, entering, later)
        right = jnp.concatenate([residual[:, cut], split_right(entering.T, 0)], axis=0)
        held[:, cut] = dot(left[...], right).astype(bf16)
        copies.append(pltpu.make_async_copy(held.at[:, cut], out.at[:, cut], sems.at[at]))
        copies[-1].start()
    for copy in copies:
        copy.wait()


def on_device(right_side, inverse, coupling, initial_guess, face_order):
    rows, width = right_side.shape[-2:]
    right_side, inverse, guess = right_side[0, 0, 0], inverse[0, 0, 0], initial_guess[0, 0, 0]
    coupling, order = coupling[0, 0, 0], face_order[0, 0, 0]
    count = lax.axis_size("stream")
    assert count == 4 * GROUP
    part = width // GROUP
    chips = [[i, i + 1] for i in range(0, count, 2)]
    near = [[g * GROUP + i for i in range(GROUP)] for g in range(4)]

    outer = pl.BlockSpec(memory_space=pltpu.HBM)
    blocks = width // (2 * WIDE)

    scalar = pl.BlockSpec(memory_space=pltpu.SMEM)
    inner = pl.BlockSpec(memory_space=pltpu.VMEM)
    place = lax.axis_index("stream").astype(jnp.int32)
    core, group = (place & 1).reshape(1), (place >> 3).reshape(1)
    assert GROUP == 8 and lax.axis_size("gy") == lax.axis_size("gz")

    traces = pl.pallas_call(
        traces_kernel,
        in_specs=[scalar, inner],
        out_shape=[jax.ShapeDtypeStruct((WIDE, width), bf16)] * FACES,
        compiler_params=params(),
        cost_estimate=pl.CostEstimate(flops=8 * 10**9, bytes_accessed=2 * rows * width, transcendentals=0),
        name="face_traces",
    )(core, guess)

    size = lax.axis_size("gy")

    def upstream(value):
        return lax.ppermute(value, "stream", [(i, i - 1) for i in range(1, count)])

    def sideways(value, axis, first):
        steps = [first if i % 2 == 0 else -first for i in range(count)]
        pairs = [
            (i * size + j, i * size + j + steps[i])
            for i in range(count)
            for j in range(size)
            if 0 <= j + steps[i] < size
        ]
        return lax.ppermute(value, ("stream", axis), pairs)

    halos = [upstream(traces[0])]
    for at, (axis, first) in enumerate((("gy", 1), ("gz", -1), ("gy", -1), ("gz", 1))):
        halos.append(sideways(traces[1 + at], axis, first))

    couple, left, picked, maps = pl.pallas_call(
        maps_kernel,
        in_specs=[scalar, inner, inner, inner],
        out_shape=[
            jax.ShapeDtypeStruct((rows, FACES * WIDE), bf16),
            jax.ShapeDtypeStruct((rows, TALL + 3 * WIDE), bf16),
            jax.ShapeDtypeStruct((WIDE, rows), bf16),
            jax.ShapeDtypeStruct((WIDE, WIDE), WIRE),
        ],
        compiler_params=params(),
        name="element_maps",
    )(core, inverse, coupling, order.reshape(6, 1, TRACE))

    partial = pl.pallas_call(
        partial_kernel,
        out_shape=jax.ShapeDtypeStruct((rows, width), f32),
        cost_estimate=pl.CostEstimate(
            flops=8 * WIDE * rows * width, bytes_accessed=6 * rows * width, transcendentals=0
        ),
        compiler_params=params(),
        name="partial_residual",
    )(right_side, couple, *(halos[at] for at in (1, 2, 0, 3)))
    maps = lax.all_gather(maps, "stream", axis_index_groups=chips)
    residual, offset = pl.pallas_call(
        offset_kernel,
        out_shape=[
            jax.ShapeDtypeStruct((TALL, width), bf16),
            jax.ShapeDtypeStruct((width, WIDE), WIRE),
        ],
        compiler_params=params(),
        name="residual_offset",
    )(partial, couple, halos[4], picked)
    offsets = lax.all_gather(offset, "stream", axis_index_groups=chips)
    sent = pl.pallas_call(
        merge_kernel,
        in_specs=[scalar, inner, inner],
        out_shape=jax.ShapeDtypeStruct((GROUP, (part + WIDE) // 2, WIDE), WIRE),
        compiler_params=params(),
        name="chip_merge",
    )(core, offsets, maps)
    received = lax.all_to_all(sent, "stream", 0, 0, tiled=True, axis_index_groups=near)
    states, total, both = pl.pallas_call(
        scan_kernel,
        out_shape=[
            jax.ShapeDtypeStruct((GROUP // 2 - 1, part + WIDE, WIDE), f32),
            jax.ShapeDtypeStruct((part, WIDE), WIRE),
            jax.ShapeDtypeStruct((part + WIDE, WIDE), WIRE),
        ],
        compiler_params=params(),
        name="group_scan",
    )(received)

    def between(value, *pairs):
        moves = [(a * GROUP + i, b * GROUP + i) for a, b in pairs for i in range(GROUP)]
        return lax.ppermute(value, "stream", moves)

    above = between(both, (1, 0))
    first = between(total, (0, 1))
    third = between(both, (2, 3))
    pair = pl.pallas_call(
        pair_kernel,
        in_specs=[scalar] + [inner] * 3,
        out_shape=jax.ShapeDtypeStruct((part, WIDE), WIRE),
        compiler_params=params(),
        name="pair_total",
    )(group, both, above, first)
    pair = between(pair, (1, 2), (0, 3))
    entering = pl.pallas_call(
        prefix_kernel,
        in_specs=[scalar] + [inner] * 4,
        out_shape=jax.ShapeDtypeStruct((GROUP, part, WIDE), WIRE),
        compiler_params=params(),
        name="group_prefix",
    )(group, first, pair, third, states)
    arrived = lax.all_to_all(entering, "stream", 0, 0, tiled=True, axis_index_groups=near)

    updated = pl.pallas_call(
        update_kernel,
        in_specs=[scalar] + [inner] * 5,
        out_specs=outer,
        out_shape=jax.ShapeDtypeStruct((rows, width), bf16),
        scratch_shapes=[pltpu.VMEM((rows, width), bf16), pltpu.SemaphoreType.DMA((blocks,))],
        compiler_params=params(),
        name="update",
    )(core, left, residual, arrived.reshape(width, WIDE), offsets, maps)
    return updated[None, None, None]


def solution(mesh):
    return jax.shard_map(
        on_device,
        mesh=mesh,
        in_specs=(
            P("stream", "gy", "gz", None, None),
            P("stream", "gy", "gz", None, None),
            P("stream", "gy", "gz", None, None, None),
            P("stream", "gy", "gz", None, None),
            P("stream", "gy", "gz", None, None),
        ),
        out_specs=P("stream", "gy", "gz", None, None),
        check_vma=False,
    )
```

```python
import jax
import jax.numpy as jnp
from jax import lax
from jax.experimental import pallas as pl
from jax.experimental.pallas import tpu as pltpu
from jax.sharding import PartitionSpec as P

NODE = 5
TRACE = 125
WIDE = 128
TALL = 640
FACES = 5
GROUP = 8
f32, bf16 = jnp.float32, jnp.bfloat16
WIRE = jnp.int16
GRANT = 40 * 1024 * 1024


def params():
    return pltpu.CompilerParams(vmem_limit_bytes=GRANT)


def dot(left, right, contract=(1, 0)):
    dims = (((contract[0],), (contract[1],)), ((), ()))
    return lax.dot_general(left, right, dims, preferred_element_type=f32)


def halves(value):
    high = value.astype(bf16)
    return high, (value - high.astype(f32)).astype(bf16)


def split_left(value):
    high, low = halves(value)
    return jnp.concatenate([high, low, high], axis=1)


def split_right(value, axis):
    high, low = halves(value)
    return jnp.concatenate([high, high, low], axis=axis)


def coded(value):
    lane = lax.broadcasted_iota(jnp.int32, value.shape, 1)
    top = jnp.max(jnp.abs(value), axis=1, keepdims=True)
    power = jnp.minimum(jnp.ceil(jnp.log2(jnp.maximum(top, 1e-30))), 127.0)
    fraction = jnp.round(value * jnp.exp2(13.9 - power))
    return jnp.where(lane == WIDE - 1, power, fraction).astype(jnp.int32).astype(WIRE)


def decoded(block):
    value = block.astype(jnp.int32).astype(f32)
    lane = lax.broadcasted_iota(jnp.int32, value.shape, 1)
    power = value[:, WIDE - 1 :]
    return jnp.where(lane == WIDE - 1, 0.0, value * jnp.exp2(power - 13.9))


def trace_rows(which, side):
    at = lax.broadcasted_iota(jnp.int32, (WIDE, 1), 0)
    var = (at * 41) >> 10
    rest = at - 25 * var
    slow = (rest * 13) >> 6
    fast = rest - 5 * slow
    place = [side, slow, fast]
    if which == 1:
        place = [slow, side, fast]
    if which == 2:
        place = [slow, fast, side]
    row = var * 125 + place[0] * 25 + place[1] * 5 + place[2]
    row = jnp.where(at < TRACE, row, -1)
    column = lax.broadcasted_iota(jnp.int32, (WIDE, 625), 1)
    return (row == column).astype(f32).astype(bf16)


def traces_kernel(core, guess, *outs):
    last = NODE - 1
    y, z = last * (1 - core[0]), last * (core[0])
    sent = ((0, 0), (1, y), (2, z), (1, last - y), (2, last - z))
    for (which, side), out in zip(sent, outs):
        out[...] = dot(trace_rows(which, side), guess[...]).astype(bf16)


def maps_kernel(core, inverse, coupling, order, couple_out, left_out, inverse_out, map_out):
    node = lax.broadcasted_iota(jnp.int32, (WIDE, TRACE), 0)

    def permuted(face):
        pick = (node == order[face]).astype(f32).astype(bf16)
        return dot(coupling[face], pick, (1, 1)).astype(bf16)

    turn = core[0]
    for at, face in enumerate((2 + turn, 5 - turn, 1, 3 - turn, 4 + turn)):
        couple_out[:, at * WIDE : (at + 1) * WIDE] = permuted(face)
    first = permuted(0)
    left_out[...] = jnp.zeros(left_out.shape, bf16)
    left_out[:, : inverse.shape[1]] = inverse[...]
    left_out[:, TALL:] = split_left(-dot(inverse[...], first))
    picked = dot(trace_rows(0, NODE - 1), inverse[...]).astype(bf16)
    inverse_out[...] = picked
    map_out[...] = coded(-dot(picked, first).T)


def partial_kernel(right_side, couple, t1, t2, t3, t4, out):
    traces = jnp.concatenate([t[...] for t in (t1, t2, t3, t4)], axis=0)
    out[...] = right_side[...].astype(f32) - dot(couple[:, : 4 * WIDE], traces)


def offset_kernel(partial, couple, t5, inverse, residual_out, offset_out):
    pulled = dot(couple[:, 4 * WIDE :], t5[...])
    residual = (partial[...] - pulled).astype(bf16)
    rows, width = residual.shape
    padding = jnp.zeros((residual_out.shape[0] - rows, width), bf16)
    residual_out[...] = jnp.concatenate([residual, padding], axis=0)
    offset_out[...] = coded(dot(inverse[...], residual).T)


def merge_kernel(core, offsets, maps, send_out):
    count, rows, _ = send_out.shape
    half = rows - WIDE // 2
    last = split_right(decoded(maps[1]), 0)
    step = dot(split_left(decoded(maps[0])), last)
    step = coded(jnp.where(core[0] == 0, step[: WIDE // 2], step[WIDE // 2 :]))

    def mine(which):
        starts = (pl.multiple_of((2 * at + core[0]) * half, 16) for at in range(count))
        return jnp.concatenate([offsets[which, pl.ds(start, half), :] for start in starts], axis=0)

    merged = coded(decoded(mine(1)) + dot(split_left(decoded(mine(0))), last))
    for at in range(count):
        send_out[at, :half, :] = merged[at * half : (at + 1) * half]
        send_out[at, half:, :] = step


def scan_kernel(received, states_out, total_out, both_out):
    count, rows, _ = received.shape
    half = rows - WIDE // 2
    part = 2 * half
    steps = []
    for at in range(0, count, 2):
        low, high = decoded(received[at]), decoded(received[at + 1])
        steps.append((low[:half], high[:half], low[half:], high[half:]))
    state = jnp.concatenate(steps[0], axis=0)
    for at in range(1, count // 2):
        states_out[at - 1] = state
        moved = dot(split_left(state), split_right(jnp.concatenate(steps[at][2:], axis=0), 0))
        offset = jnp.concatenate(steps[at][:2], axis=0)
        state = jnp.concatenate([moved[:part] + offset, moved[part:]], axis=0)
    whole = coded(state)
    total_out[...] = whole[:part]
    both_out[...] = whole


def passed(entering, state):
    part = entering.shape[0]
    return state[:part] + dot(split_left(entering), split_right(state[part:], 0))


def pair_kernel(group, own, above, below, out):
    part = out.shape[0]
    first = group[0] == 0
    mine = decoded(own[...])
    state = jnp.where(first, decoded(above[...]), mine)
    entering = jnp.where(first, mine[:part], decoded(below[...]))
    out[...] = coded(passed(entering, state))


def prefix_kernel(group, first, pair, third, states, solved, out):
    count, part, _ = out.shape
    entering = decoded(pair[...])
    later = passed(entering, decoded(third[...]))
    entering = jnp.where(group[0] == 3, later, entering) + decoded(first[...])
    left = split_left(entering)
    for at in range(0, count, 2):
        value = entering
        if at > 0:
            state = states[at // 2 - 1]
            value = state[:part] + dot(left, split_right(state[part:], 0))
        value = coded(value)
        out[at] = value
        out[at + 1] = value


def solve_kernel(core, left, residual, offsets, maps, solved_out, gain_out):
    later = core[0] == 1
    offset = jnp.where(later, decoded(offsets[0]), 0.0)
    right = jnp.concatenate([residual[...], split_right(offset.T, 0)], axis=0)
    solved_out[...] = dot(left[...], right)
    gain = left[:, TALL:]
    own = gain[:, :WIDE].astype(f32) + gain[:, WIDE : 2 * WIDE].astype(f32)
    through = dot(gain, split_right(decoded(maps[0]).T, 0))
    gain_out[...] = split_left(jnp.where(later, through, own))


def update_kernel(solved, gain, arrived, out, held, sems):
    block = held.shape[1] // sems.shape[0]
    copies = []
    for at in range(sems.shape[0]):
        cut = slice(at * block, (at + 1) * block)
        moved = dot(gain[...], split_right(decoded(arrived[cut, :]).T, 0))
        held[:, cut] = (solved[:, cut] + moved).astype(bf16)
        copies.append(pltpu.make_async_copy(held.at[:, cut], out.at[:, cut], sems.at[at]))
        copies[-1].start()
    for copy in copies:
        copy.wait()


def on_device(right_side, inverse, coupling, initial_guess, face_order):
    rows, width = right_side.shape[-2:]
    right_side, inverse, guess = right_side[0, 0, 0], inverse[0, 0, 0], initial_guess[0, 0, 0]
    coupling, order = coupling[0, 0, 0], face_order[0, 0, 0]
    count = lax.axis_size("stream")
    assert count == 4 * GROUP
    part = width // GROUP
    chips = [[i, i + 1] for i in range(0, count, 2)]
    near = [[g * GROUP + i for i in range(GROUP)] for g in range(4)]

    outer = pl.BlockSpec(memory_space=pltpu.HBM)

    scalar = pl.BlockSpec(memory_space=pltpu.SMEM)
    inner = pl.BlockSpec(memory_space=pltpu.VMEM)
    place = lax.axis_index("stream").astype(jnp.int32)
    core, group = (place & 1).reshape(1), (place >> 3).reshape(1)
    assert GROUP == 8 and lax.axis_size("gy") == lax.axis_size("gz")

    traces = pl.pallas_call(
        traces_kernel,
        in_specs=[scalar, inner],
        out_shape=[jax.ShapeDtypeStruct((WIDE, width), bf16)] * FACES,
        compiler_params=params(),
        cost_estimate=pl.CostEstimate(flops=8 * 10**9, bytes_accessed=2 * rows * width, transcendentals=0),
        name="face_traces",
    )(core, guess)

    size = lax.axis_size("gy")

    def upstream(value):
        return lax.ppermute(value, "stream", [(i, i - 1) for i in range(1, count)])

    def sideways(value, axis, first):
        steps = [first if i % 2 == 0 else -first for i in range(count)]
        pairs = [
            (i * size + j, i * size + j + steps[i])
            for i in range(count)
            for j in range(size)
            if 0 <= j + steps[i] < size
        ]
        return lax.ppermute(value, ("stream", axis), pairs)

    halos = [upstream(traces[0])]
    for at, (axis, first) in enumerate((("gy", 1), ("gz", -1), ("gy", -1), ("gz", 1))):
        halos.append(sideways(traces[1 + at], axis, first))

    couple, left, picked, maps = pl.pallas_call(
        maps_kernel,
        in_specs=[scalar, inner, inner, inner],
        out_shape=[
            jax.ShapeDtypeStruct((rows, FACES * WIDE), bf16),
            jax.ShapeDtypeStruct((rows, TALL + 3 * WIDE), bf16),
            jax.ShapeDtypeStruct((WIDE, rows), bf16),
            jax.ShapeDtypeStruct((WIDE, WIDE), WIRE),
        ],
        compiler_params=params(),
        name="element_maps",
    )(core, inverse, coupling, order.reshape(6, 1, TRACE))

    partial = pl.pallas_call(
        partial_kernel,
        out_shape=jax.ShapeDtypeStruct((rows, width), f32),
        cost_estimate=pl.CostEstimate(
            flops=8 * WIDE * rows * width, bytes_accessed=6 * rows * width, transcendentals=0
        ),
        compiler_params=params(),
        name="partial_residual",
    )(right_side, couple, *(halos[at] for at in (1, 2, 0, 3)))
    maps = lax.all_gather(maps, "stream", axis_index_groups=chips)
    residual, offset = pl.pallas_call(
        offset_kernel,
        out_shape=[
            jax.ShapeDtypeStruct((TALL, width), bf16),
            jax.ShapeDtypeStruct((width, WIDE), WIRE),
        ],
        compiler_params=params(),
        name="residual_offset",
    )(partial, couple, halos[4], picked)
    offsets = lax.all_gather(offset, "stream", axis_index_groups=chips)
    sent = pl.pallas_call(
        merge_kernel,
        in_specs=[scalar, inner, inner],
        out_shape=jax.ShapeDtypeStruct((GROUP, (part + WIDE) // 2, WIDE), WIRE),
        compiler_params=params(),
        name="chip_merge",
    )(core, offsets, maps)
    received = lax.all_to_all(sent, "stream", 0, 0, tiled=True, axis_index_groups=near)
    states, total, both = pl.pallas_call(
        scan_kernel,
        out_shape=[
            jax.ShapeDtypeStruct((GROUP // 2 - 1, part + WIDE, WIDE), f32),
            jax.ShapeDtypeStruct((part, WIDE), WIRE),
            jax.ShapeDtypeStruct((part + WIDE, WIDE), WIRE),
        ],
        compiler_params=params(),
        name="group_scan",
    )(received)

    def between(value, *pairs):
        moves = [(a * GROUP + i, b * GROUP + i) for a, b in pairs for i in range(GROUP)]
        return lax.ppermute(value, "stream", moves)

    above = between(both, (1, 0))
    first = between(total, (0, 1))
    third = between(both, (2, 3))
    solved, gain = pl.pallas_call(
        solve_kernel,
        in_specs=[scalar] + [inner] * 4,
        out_shape=[
            jax.ShapeDtypeStruct((rows, width), f32),
            jax.ShapeDtypeStruct((rows, 3 * WIDE), bf16),
        ],
        cost_estimate=pl.CostEstimate(
            flops=2 * rows * 1024 * width, bytes_accessed=4 * rows * width, transcendentals=0
        ),
        compiler_params=params(),
        name="solve",
    )(core, left, residual, offsets, maps)
    pair = pl.pallas_call(
        pair_kernel,
        in_specs=[scalar] + [inner] * 3,
        out_shape=jax.ShapeDtypeStruct((part, WIDE), WIRE),
        compiler_params=params(),
        name="pair_total",
    )(group, both, above, first)
    pair = between(pair, (1, 2), (0, 3))
    entering = pl.pallas_call(
        prefix_kernel,
        in_specs=[scalar] + [inner] * 5,
        out_shape=jax.ShapeDtypeStruct((GROUP, part, WIDE), WIRE),
        compiler_params=params(),
        name="group_prefix",
    )(group, first, pair, third, states, solved)
    arrived = lax.all_to_all(entering, "stream", 0, 0, tiled=True, axis_index_groups=near)

    updated = pl.pallas_call(
        update_kernel,
        in_specs=[inner] * 3,
        out_specs=outer,
        out_shape=jax.ShapeDtypeStruct((rows, width), bf16),
        scratch_shapes=[pltpu.VMEM((rows, width), bf16), pltpu.SemaphoreType.DMA((3,))],
        compiler_params=params(),
        name="update",
    )(solved, gain, arrived.reshape(width, WIDE))
    return updated[None, None, None]


def solution(mesh):
    return jax.shard_map(
        on_device,
        mesh=mesh,
        in_specs=(
            P("stream", "gy", "gz", None, None),
            P("stream", "gy", "gz", None, None),
            P("stream", "gy", "gz", None, None, None),
            P("stream", "gy", "gz", None, None),
            P("stream", "gy", "gz", None, None),
        ),
        out_specs=P("stream", "gy", "gz", None, None),
        check_vma=False,
    )
```

```python
import jax
import jax.numpy as jnp
from jax import lax
from jax.experimental import pallas as pl
from jax.experimental.pallas import tpu as pltpu
from jax.sharding import PartitionSpec as P

NODE = 5
TRACE = 125
WIDE = 128
TALL = 640
FACES = 5
GROUP = 8
f32, bf16 = jnp.float32, jnp.bfloat16
WIRE = jnp.int16
GRANT = 40 * 1024 * 1024


def params():
    return pltpu.CompilerParams(vmem_limit_bytes=GRANT)


def dot(left, right, contract=(1, 0)):
    dims = (((contract[0],), (contract[1],)), ((), ()))
    return lax.dot_general(left, right, dims, preferred_element_type=f32)


def halves(value):
    high = value.astype(bf16)
    return high, (value - high.astype(f32)).astype(bf16)


def split_left(value):
    high, low = halves(value)
    return jnp.concatenate([high, low, high], axis=1)


def split_right(value, axis):
    high, low = halves(value)
    return jnp.concatenate([high, high, low], axis=axis)


def coded(value):
    lane = lax.broadcasted_iota(jnp.int32, value.shape, 1)
    top = jnp.max(jnp.abs(value), axis=1, keepdims=True)
    power = jnp.minimum(jnp.ceil(jnp.log2(jnp.maximum(top, 1e-30))), 127.0)
    fraction = jnp.round(value * jnp.exp2(13.9 - power))
    return jnp.where(lane == WIDE - 1, power, fraction).astype(jnp.int32).astype(WIRE)


def decoded(block):
    value = block.astype(jnp.int32).astype(f32)
    lane = lax.broadcasted_iota(jnp.int32, value.shape, 1)
    power = value[:, WIDE - 1 :]
    return jnp.where(lane == WIDE - 1, 0.0, value * jnp.exp2(power - 13.9))


def trace_rows(which, side):
    at = lax.broadcasted_iota(jnp.int32, (WIDE, 1), 0)
    var = (at * 41) >> 10
    rest = at - 25 * var
    slow = (rest * 13) >> 6
    fast = rest - 5 * slow
    place = [side, slow, fast]
    if which == 1:
        place = [slow, side, fast]
    if which == 2:
        place = [slow, fast, side]
    row = var * 125 + place[0] * 25 + place[1] * 5 + place[2]
    row = jnp.where(at < TRACE, row, -1)
    column = lax.broadcasted_iota(jnp.int32, (WIDE, 625), 1)
    return (row == column).astype(f32).astype(bf16)


def traces_kernel(core, guess, *outs):
    last = NODE - 1
    y, z = last * (1 - core[0]), last * (core[0])
    sent = ((0, 0), (1, y), (2, z), (1, last - y), (2, last - z))
    for (which, side), out in zip(sent, outs):
        out[...] = dot(trace_rows(which, side), guess[...]).astype(bf16)


def maps_kernel(core, inverse, coupling, order, couple_out, left_out, inverse_out, map_out):
    node = lax.broadcasted_iota(jnp.int32, (WIDE, TRACE), 0)

    def permuted(face):
        pick = (node == order[face]).astype(f32).astype(bf16)
        return dot(coupling[face], pick, (1, 1)).astype(bf16)

    turn = core[0]
    for at, face in enumerate((2 + turn, 5 - turn, 1, 3 - turn, 4 + turn)):
        couple_out[:, at * WIDE : (at + 1) * WIDE] = permuted(face)
    first = permuted(0)
    left_out[...] = jnp.zeros(left_out.shape, bf16)
    left_out[:, : inverse.shape[1]] = inverse[...]
    left_out[:, TALL:] = split_left(-dot(inverse[...], first))
    picked = dot(trace_rows(0, NODE - 1), inverse[...]).astype(bf16)
    inverse_out[...] = picked
    map_out[...] = coded(-dot(picked, first).T)


def partial_kernel(right_side, couple, t1, t2, t3, t4, out):
    traces = jnp.concatenate([t[...] for t in (t1, t2, t3, t4)], axis=0)
    out[...] = right_side[...].astype(f32) - dot(couple[:, : 4 * WIDE], traces)


def offset_kernel(partial, couple, t5, inverse, maps, residual_out, offset_out):
    pulled = dot(couple[:, 4 * WIDE :], t5[...])
    residual = (partial[...] - pulled).astype(bf16)
    rows, width = residual.shape
    padding = jnp.zeros((residual_out.shape[0] - rows, width), bf16)
    residual_out[...] = jnp.concatenate([residual, padding], axis=0)
    offset_out[:width, :] = coded(dot(inverse[...], residual).T)
    offset_out[width:, :] = maps[...]


def merge_kernel(core, offsets, send_out):
    count, rows, _ = send_out.shape
    half = rows - WIDE // 2
    width = 2 * count * half
    last = split_right(decoded(offsets[1, width:, :]), 0)
    step = dot(split_left(decoded(offsets[0, width:, :])), last)
    step = coded(jnp.where(core[0] == 0, step[: WIDE // 2], step[WIDE // 2 :]))

    def mine(which):
        starts = (pl.multiple_of((2 * at + core[0]) * half, 16) for at in range(count))
        return jnp.concatenate([offsets[which, pl.ds(start, half), :] for start in starts], axis=0)

    merged = coded(decoded(mine(1)) + dot(split_left(decoded(mine(0))), last))
    for at in range(count):
        send_out[at, :half, :] = merged[at * half : (at + 1) * half]
        send_out[at, half:, :] = step


def scan_kernel(received, states_out, total_out, both_out):
    count, rows, _ = received.shape
    half = rows - WIDE // 2
    part = 2 * half
    steps = []
    for at in range(0, count, 2):
        low, high = decoded(received[at]), decoded(received[at + 1])
        steps.append((low[:half], high[:half], low[half:], high[half:]))
    state = jnp.concatenate(steps[0], axis=0)
    for at in range(1, count // 2):
        states_out[at - 1] = state
        moved = dot(split_left(state), split_right(jnp.concatenate(steps[at][2:], axis=0), 0))
        offset = jnp.concatenate(steps[at][:2], axis=0)
        state = jnp.concatenate([moved[:part] + offset, moved[part:]], axis=0)
    whole = coded(state)
    total_out[...] = whole[:part]
    both_out[...] = whole


def passed(entering, state):
    part = entering.shape[0]
    return state[:part] + dot(split_left(entering), split_right(state[part:], 0))


def pair_kernel(group, own, above, below, out):
    part = out.shape[0]
    first = group[0] == 0
    mine = decoded(own[...])
    state = jnp.where(first, decoded(above[...]), mine)
    entering = jnp.where(first, mine[:part], decoded(below[...]))
    out[...] = coded(passed(entering, state))


def prefix_kernel(group, first, pair, third, states, solved, out):
    count, part, _ = out.shape
    entering = decoded(pair[...])
    later = passed(entering, decoded(third[...]))
    entering = jnp.where(group[0] == 3, later, entering) + decoded(first[...])
    left = split_left(entering)
    for at in range(0, count, 2):
        value = entering
        if at > 0:
            state = states[at // 2 - 1]
            value = state[:part] + dot(left, split_right(state[part:], 0))
        value = coded(value)
        out[at] = value
        out[at + 1] = value


def solve_kernel(core, left, residual, offsets, solved_out, gain_out):
    later = core[0] == 1
    width = residual.shape[1]
    offset = jnp.where(later, decoded(offsets[0, :width, :]), 0.0)
    right = jnp.concatenate([residual[...], split_right(offset.T, 0)], axis=0)
    solved_out[...] = dot(left[...], right)
    gain = left[:, TALL:]
    own = gain[:, :WIDE].astype(f32) + gain[:, WIDE : 2 * WIDE].astype(f32)
    through = dot(gain, split_right(decoded(offsets[0, width:, :]).T, 0))
    gain_out[...] = split_left(jnp.where(later, through, own))


def update_kernel(solved, gain, arrived, out, held, sems):
    block = held.shape[1] // sems.shape[0]
    copies = []
    for at in range(sems.shape[0]):
        cut = slice(at * block, (at + 1) * block)
        moved = dot(gain[...], split_right(decoded(arrived[cut, :]).T, 0))
        held[:, cut] = (solved[:, cut] + moved).astype(bf16)
        copies.append(pltpu.make_async_copy(held.at[:, cut], out.at[:, cut], sems.at[at]))
        copies[-1].start()
    for copy in copies:
        copy.wait()


def on_device(right_side, inverse, coupling, initial_guess, face_order):
    rows, width = right_side.shape[-2:]
    right_side, inverse, guess = right_side[0, 0, 0], inverse[0, 0, 0], initial_guess[0, 0, 0]
    coupling, order = coupling[0, 0, 0], face_order[0, 0, 0]
    count = lax.axis_size("stream")
    assert count == 4 * GROUP
    part = width // GROUP
    chips = [[i, i + 1] for i in range(0, count, 2)]
    near = [[g * GROUP + i for i in range(GROUP)] for g in range(4)]

    outer = pl.BlockSpec(memory_space=pltpu.HBM)

    scalar = pl.BlockSpec(memory_space=pltpu.SMEM)
    inner = pl.BlockSpec(memory_space=pltpu.VMEM)
    place = lax.axis_index("stream").astype(jnp.int32)
    core, group = (place & 1).reshape(1), (place >> 3).reshape(1)
    assert GROUP == 8 and lax.axis_size("gy") == lax.axis_size("gz")

    traces = pl.pallas_call(
        traces_kernel,
        in_specs=[scalar, inner],
        out_shape=[jax.ShapeDtypeStruct((WIDE, width), bf16)] * FACES,
        compiler_params=params(),
        cost_estimate=pl.CostEstimate(flops=8 * 10**9, bytes_accessed=2 * rows * width, transcendentals=0),
        name="face_traces",
    )(core, guess)

    size = lax.axis_size("gy")

    def upstream(value):
        return lax.ppermute(value, "stream", [(i, i - 1) for i in range(1, count)])

    def sideways(value, axis, first):
        steps = [first if i % 2 == 0 else -first for i in range(count)]
        pairs = [
            (i * size + j, i * size + j + steps[i])
            for i in range(count)
            for j in range(size)
            if 0 <= j + steps[i] < size
        ]
        return lax.ppermute(value, ("stream", axis), pairs)

    halos = [upstream(traces[0])]
    for at, (axis, first) in enumerate((("gy", 1), ("gz", -1), ("gy", -1), ("gz", 1))):
        halos.append(sideways(traces[1 + at], axis, first))

    couple, left, picked, maps = pl.pallas_call(
        maps_kernel,
        in_specs=[scalar, inner, inner, inner],
        out_shape=[
            jax.ShapeDtypeStruct((rows, FACES * WIDE), bf16),
            jax.ShapeDtypeStruct((rows, TALL + 3 * WIDE), bf16),
            jax.ShapeDtypeStruct((WIDE, rows), bf16),
            jax.ShapeDtypeStruct((WIDE, WIDE), WIRE),
        ],
        compiler_params=params(),
        name="element_maps",
    )(core, inverse, coupling, order.reshape(6, 1, TRACE))

    partial = pl.pallas_call(
        partial_kernel,
        out_shape=jax.ShapeDtypeStruct((rows, width), f32),
        cost_estimate=pl.CostEstimate(
            flops=8 * WIDE * rows * width, bytes_accessed=6 * rows * width, transcendentals=0
        ),
        compiler_params=params(),
        name="partial_residual",
    )(right_side, couple, *(halos[at] for at in (1, 2, 0, 3)))
    residual, offset = pl.pallas_call(
        offset_kernel,
        out_shape=[
            jax.ShapeDtypeStruct((TALL, width), bf16),
            jax.ShapeDtypeStruct((width + WIDE, WIDE), WIRE),
        ],
        compiler_params=params(),
        name="residual_offset",
    )(partial, couple, halos[4], picked, maps)
    offsets = lax.all_gather(offset, "stream", axis_index_groups=chips)
    sent = pl.pallas_call(
        merge_kernel,
        in_specs=[scalar, inner],
        out_shape=jax.ShapeDtypeStruct((GROUP, (part + WIDE) // 2, WIDE), WIRE),
        compiler_params=params(),
        name="chip_merge",
    )(core, offsets)
    received = lax.all_to_all(sent, "stream", 0, 0, tiled=True, axis_index_groups=near)
    states, total, both = pl.pallas_call(
        scan_kernel,
        out_shape=[
            jax.ShapeDtypeStruct((GROUP // 2 - 1, part + WIDE, WIDE), f32),
            jax.ShapeDtypeStruct((part, WIDE), WIRE),
            jax.ShapeDtypeStruct((part + WIDE, WIDE), WIRE),
        ],
        compiler_params=params(),
        name="group_scan",
    )(received)

    def between(value, *pairs):
        moves = [(a * GROUP + i, b * GROUP + i) for a, b in pairs for i in range(GROUP)]
        return lax.ppermute(value, "stream", moves)

    above = between(both, (1, 0))
    first = between(total, (0, 1))
    third = between(both, (2, 3))
    solved, gain = pl.pallas_call(
        solve_kernel,
        in_specs=[scalar] + [inner] * 3,
        out_shape=[
            jax.ShapeDtypeStruct((rows, width), f32),
            jax.ShapeDtypeStruct((rows, 3 * WIDE), bf16),
        ],
        cost_estimate=pl.CostEstimate(
            flops=2 * rows * 1024 * width, bytes_accessed=4 * rows * width, transcendentals=0
        ),
        compiler_params=params(),
        name="solve",
    )(core, left, residual, offsets)
    pair = pl.pallas_call(
        pair_kernel,
        in_specs=[scalar] + [inner] * 3,
        out_shape=jax.ShapeDtypeStruct((part, WIDE), WIRE),
        compiler_params=params(),
        name="pair_total",
    )(group, both, above, first)
    pair = between(pair, (1, 2), (0, 3))
    entering = pl.pallas_call(
        prefix_kernel,
        in_specs=[scalar] + [inner] * 5,
        out_shape=jax.ShapeDtypeStruct((GROUP, part, WIDE), WIRE),
        compiler_params=params(),
        name="group_prefix",
    )(group, first, pair, third, states, solved)
    arrived = lax.all_to_all(entering, "stream", 0, 0, tiled=True, axis_index_groups=near)

    updated = pl.pallas_call(
        update_kernel,
        in_specs=[inner] * 3,
        out_specs=outer,
        out_shape=jax.ShapeDtypeStruct((rows, width), bf16),
        scratch_shapes=[pltpu.VMEM((rows, width), bf16), pltpu.SemaphoreType.DMA((3,))],
        compiler_params=params(),
        name="update",
    )(solved, gain, arrived.reshape(width, WIDE))
    return updated[None, None, None]


def solution(mesh):
    return jax.shard_map(
        on_device,
        mesh=mesh,
        in_specs=(
            P("stream", "gy", "gz", None, None),
            P("stream", "gy", "gz", None, None),
            P("stream", "gy", "gz", None, None, None),
            P("stream", "gy", "gz", None, None),
            P("stream", "gy", "gz", None, None),
        ),
        out_specs=P("stream", "gy", "gz", None, None),
        check_vma=False,
    )
```

```python
import jax
import jax.numpy as jnp
from jax import lax
from jax.experimental import pallas as pl
from jax.experimental.pallas import tpu as pltpu
from jax.sharding import PartitionSpec as P

NODE = 5
TRACE = 125
WIDE = 128
TALL = 640
FACES = 5
GROUP = 8
f32, bf16 = jnp.float32, jnp.bfloat16
WIRE = jnp.int16
GRANT = 40 * 1024 * 1024


def params():
    return pltpu.CompilerParams(vmem_limit_bytes=GRANT)


def dot(left, right, contract=(1, 0)):
    dims = (((contract[0],), (contract[1],)), ((), ()))
    return lax.dot_general(left, right, dims, preferred_element_type=f32)


def halves(value):
    high = value.astype(bf16)
    return high, (value - high.astype(f32)).astype(bf16)


def split_left(value):
    high, low = halves(value)
    return jnp.concatenate([high, low, high], axis=1)


def split_right(value, axis):
    high, low = halves(value)
    return jnp.concatenate([high, high, low], axis=axis)


def coded(value):
    lane = lax.broadcasted_iota(jnp.int32, value.shape, 1)
    top = jnp.max(jnp.abs(value), axis=1, keepdims=True)
    power = jnp.minimum(jnp.ceil(jnp.log2(jnp.maximum(top, 1e-30))), 127.0)
    fraction = jnp.round(value * jnp.exp2(13.9 - power))
    return jnp.where(lane == WIDE - 1, power, fraction).astype(jnp.int32).astype(WIRE)


def decoded(block):
    value = block.astype(jnp.int32).astype(f32)
    lane = lax.broadcasted_iota(jnp.int32, value.shape, 1)
    power = value[:, WIDE - 1 :]
    return jnp.where(lane == WIDE - 1, 0.0, value * jnp.exp2(power - 13.9))


def trace_rows(which, side):
    at = lax.broadcasted_iota(jnp.int32, (WIDE, 1), 0)
    var = (at * 41) >> 10
    rest = at - 25 * var
    slow = (rest * 13) >> 6
    fast = rest - 5 * slow
    place = [side, slow, fast]
    if which == 1:
        place = [slow, side, fast]
    if which == 2:
        place = [slow, fast, side]
    row = var * 125 + place[0] * 25 + place[1] * 5 + place[2]
    row = jnp.where(at < TRACE, row, -1)
    column = lax.broadcasted_iota(jnp.int32, (WIDE, 625), 1)
    return (row == column).astype(f32).astype(bf16)


def traces_kernel(core, guess, *outs):
    last = NODE - 1
    y, z = last * (1 - core[0]), last * (core[0])
    sent = ((0, 0), (1, y), (2, z), (1, last - y), (2, last - z))
    for (which, side), out in zip(sent, outs):
        out[...] = dot(trace_rows(which, side), guess[...]).astype(bf16)


def maps_kernel(core, inverse, coupling, order, couple_out, left_out, inverse_out, map_out):
    node = lax.broadcasted_iota(jnp.int32, (WIDE, TRACE), 0)

    def permuted(face):
        pick = (node == order[face]).astype(f32).astype(bf16)
        return dot(coupling[face], pick, (1, 1)).astype(bf16)

    turn = core[0]
    for at, face in enumerate((1, 2 + turn, 5 - turn, 3 - turn, 4 + turn)):
        couple_out[:, at * WIDE : (at + 1) * WIDE] = permuted(face)
    first = permuted(0)
    left_out[...] = jnp.zeros(left_out.shape, bf16)
    left_out[:, : inverse.shape[1]] = inverse[...]
    left_out[:, TALL:] = split_left(-dot(inverse[...], first))
    picked = dot(trace_rows(0, NODE - 1), inverse[...]).astype(bf16)
    inverse_out[...] = picked
    map_out[...] = coded(-dot(picked, first).T)


def partial_kernel(right_side, couple, t1, t2, t3, t4, out):
    traces = jnp.concatenate([t[...] for t in (t1, t2, t3, t4)], axis=0)
    out[...] = right_side[...].astype(f32) - dot(couple[:, : 4 * WIDE], traces)


def offset_kernel(partial, couple, t5, inverse, maps, residual_out, offset_out):
    pulled = dot(couple[:, 4 * WIDE :], t5[...])
    residual = (partial[...] - pulled).astype(bf16)
    rows, width = residual.shape
    padding = jnp.zeros((residual_out.shape[0] - rows, width), bf16)
    residual_out[...] = jnp.concatenate([residual, padding], axis=0)
    offset_out[:width, :] = coded(dot(inverse[...], residual).T)
    offset_out[width:, :] = maps[...]


def merge_kernel(core, offsets, send_out):
    count, rows, _ = send_out.shape
    half = rows - WIDE // 2
    width = 2 * count * half
    last = split_right(decoded(offsets[1, width:, :]), 0)
    step = dot(split_left(decoded(offsets[0, width:, :])), last)
    step = coded(jnp.where(core[0] == 0, step[: WIDE // 2], step[WIDE // 2 :]))

    def mine(which):
        starts = (pl.multiple_of((2 * at + core[0]) * half, 16) for at in range(count))
        return jnp.concatenate([offsets[which, pl.ds(start, half), :] for start in starts], axis=0)

    merged = coded(decoded(mine(1)) + dot(split_left(decoded(mine(0))), last))
    for at in range(count):
        send_out[at, :half, :] = merged[at * half : (at + 1) * half]
        send_out[at, half:, :] = step


def scan_kernel(received, states_out, total_out, both_out):
    count, rows, _ = received.shape
    half = rows - WIDE // 2
    part = 2 * half
    steps = []
    for at in range(0, count, 2):
        low, high = decoded(received[at]), decoded(received[at + 1])
        steps.append((low[:half], high[:half], low[half:], high[half:]))
    state = jnp.concatenate(steps[0], axis=0)
    for at in range(1, count // 2):
        states_out[at - 1] = state
        moved = dot(split_left(state), split_right(jnp.concatenate(steps[at][2:], axis=0), 0))
        offset = jnp.concatenate(steps[at][:2], axis=0)
        state = jnp.concatenate([moved[:part] + offset, moved[part:]], axis=0)
    whole = coded(state)
    total_out[...] = whole[:part]
    both_out[...] = whole


def passed(entering, state):
    part = entering.shape[0]
    return state[:part] + dot(split_left(entering), split_right(state[part:], 0))


def pair_kernel(group, own, above, below, out):
    part = out.shape[0]
    first = group[0] == 0
    mine = decoded(own[...])
    state = jnp.where(first, decoded(above[...]), mine)
    entering = jnp.where(first, mine[:part], decoded(below[...]))
    out[...] = coded(passed(entering, state))


def prefix_kernel(group, first, pair, third, states, solved, out):
    count, part, _ = out.shape
    entering = decoded(pair[...])
    later = passed(entering, decoded(third[...]))
    entering = jnp.where(group[0] == 3, later, entering) + decoded(first[...])
    left = split_left(entering)
    for at in range(0, count, 2):
        value = entering
        if at > 0:
            state = states[at // 2 - 1]
            value = state[:part] + dot(left, split_right(state[part:], 0))
        value = coded(value)
        out[at] = value
        out[at + 1] = value


def solve_kernel(core, left, residual, offsets, solved_out, gain_out):
    later = core[0] == 1
    width = residual.shape[1]
    offset = jnp.where(later, decoded(offsets[0, :width, :]), 0.0)
    right = jnp.concatenate([residual[...], split_right(offset.T, 0)], axis=0)
    solved_out[...] = dot(left[...], right)
    gain = left[:, TALL:]
    own = gain[:, :WIDE].astype(f32) + gain[:, WIDE : 2 * WIDE].astype(f32)
    through = dot(gain, split_right(decoded(offsets[0, width:, :]).T, 0))
    gain_out[...] = split_left(jnp.where(later, through, own))


def update_kernel(solved, gain, arrived, out, held, sems):
    block = held.shape[1] // sems.shape[0]
    copies = []
    for at in range(sems.shape[0]):
        cut = slice(at * block, (at + 1) * block)
        moved = dot(gain[...], split_right(decoded(arrived[cut, :]).T, 0))
        held[:, cut] = (solved[:, cut] + moved).astype(bf16)
        copies.append(pltpu.make_async_copy(held.at[:, cut], out.at[:, cut], sems.at[at]))
        copies[-1].start()
    for copy in copies:
        copy.wait()


def on_device(right_side, inverse, coupling, initial_guess, face_order):
    rows, width = right_side.shape[-2:]
    right_side, inverse, guess = right_side[0, 0, 0], inverse[0, 0, 0], initial_guess[0, 0, 0]
    coupling, order = coupling[0, 0, 0], face_order[0, 0, 0]
    count = lax.axis_size("stream")
    assert count == 4 * GROUP
    part = width // GROUP
    chips = [[i, i + 1] for i in range(0, count, 2)]
    near = [[g * GROUP + i for i in range(GROUP)] for g in range(4)]

    outer = pl.BlockSpec(memory_space=pltpu.HBM)

    scalar = pl.BlockSpec(memory_space=pltpu.SMEM)
    inner = pl.BlockSpec(memory_space=pltpu.VMEM)
    place = lax.axis_index("stream").astype(jnp.int32)
    core, group = (place & 1).reshape(1), (place >> 3).reshape(1)
    assert GROUP == 8 and lax.axis_size("gy") == lax.axis_size("gz")

    traces = pl.pallas_call(
        traces_kernel,
        in_specs=[scalar, inner],
        out_shape=[jax.ShapeDtypeStruct((WIDE, width), bf16)] * FACES,
        compiler_params=params(),
        cost_estimate=pl.CostEstimate(flops=8 * 10**9, bytes_accessed=2 * rows * width, transcendentals=0),
        name="face_traces",
    )(core, guess)

    size = lax.axis_size("gy")

    def upstream(value):
        return lax.ppermute(value, "stream", [(i, i - 1) for i in range(1, count)])

    def sideways(value, axis, first):
        steps = [first if i % 2 == 0 else -first for i in range(count)]
        pairs = [
            (i * size + j, i * size + j + steps[i])
            for i in range(count)
            for j in range(size)
            if 0 <= j + steps[i] < size
        ]
        return lax.ppermute(value, ("stream", axis), pairs)

    halos = [upstream(traces[0])]
    for at, (axis, first) in enumerate((("gy", 1), ("gz", -1), ("gy", -1), ("gz", 1))):
        halos.append(sideways(traces[1 + at], axis, first))

    couple, left, picked, maps = pl.pallas_call(
        maps_kernel,
        in_specs=[scalar, inner, inner, inner],
        out_shape=[
            jax.ShapeDtypeStruct((rows, FACES * WIDE), bf16),
            jax.ShapeDtypeStruct((rows, TALL + 3 * WIDE), bf16),
            jax.ShapeDtypeStruct((WIDE, rows), bf16),
            jax.ShapeDtypeStruct((WIDE, WIDE), WIRE),
        ],
        compiler_params=params(),
        name="element_maps",
    )(core, inverse, coupling, order.reshape(6, 1, TRACE))

    partial = pl.pallas_call(
        partial_kernel,
        out_shape=jax.ShapeDtypeStruct((rows, width), f32),
        cost_estimate=pl.CostEstimate(
            flops=8 * WIDE * rows * width, bytes_accessed=6 * rows * width, transcendentals=0
        ),
        compiler_params=params(),
        name="partial_residual",
    )(right_side, couple, *(halos[at] for at in (0, 1, 2, 3)))
    residual, offset = pl.pallas_call(
        offset_kernel,
        out_shape=[
            jax.ShapeDtypeStruct((TALL, width), bf16),
            jax.ShapeDtypeStruct((width + WIDE, WIDE), WIRE),
        ],
        compiler_params=params(),
        name="residual_offset",
    )(partial, couple, halos[4], picked, maps)
    offsets = lax.all_gather(offset, "stream", axis_index_groups=chips)
    sent = pl.pallas_call(
        merge_kernel,
        in_specs=[scalar, inner],
        out_shape=jax.ShapeDtypeStruct((GROUP, (part + WIDE) // 2, WIDE), WIRE),
        compiler_params=params(),
        name="chip_merge",
    )(core, offsets)
    received = lax.all_to_all(sent, "stream", 0, 0, tiled=True, axis_index_groups=near)
    states, total, both = pl.pallas_call(
        scan_kernel,
        out_shape=[
            jax.ShapeDtypeStruct((GROUP // 2 - 1, part + WIDE, WIDE), f32),
            jax.ShapeDtypeStruct((part, WIDE), WIRE),
            jax.ShapeDtypeStruct((part + WIDE, WIDE), WIRE),
        ],
        compiler_params=params(),
        name="group_scan",
    )(received)

    def between(value, *pairs):
        moves = [(a * GROUP + i, b * GROUP + i) for a, b in pairs for i in range(GROUP)]
        return lax.ppermute(value, "stream", moves)

    above = between(both, (1, 0))
    first = between(total, (0, 1))
    third = between(both, (2, 3))
    solved, gain = pl.pallas_call(
        solve_kernel,
        in_specs=[scalar] + [inner] * 3,
        out_shape=[
            jax.ShapeDtypeStruct((rows, width), f32),
            jax.ShapeDtypeStruct((rows, 3 * WIDE), bf16),
        ],
        cost_estimate=pl.CostEstimate(
            flops=2 * rows * 1024 * width, bytes_accessed=4 * rows * width, transcendentals=0
        ),
        compiler_params=params(),
        name="solve",
    )(core, left, residual, offsets)
    pair = pl.pallas_call(
        pair_kernel,
        in_specs=[scalar] + [inner] * 3,
        out_shape=jax.ShapeDtypeStruct((part, WIDE), WIRE),
        compiler_params=params(),
        name="pair_total",
    )(group, both, above, first)
    pair = between(pair, (1, 2), (0, 3))
    entering = pl.pallas_call(
        prefix_kernel,
        in_specs=[scalar] + [inner] * 5,
        out_shape=jax.ShapeDtypeStruct((GROUP, part, WIDE), WIRE),
        compiler_params=params(),
        name="group_prefix",
    )(group, first, pair, third, states, solved)
    arrived = lax.all_to_all(entering, "stream", 0, 0, tiled=True, axis_index_groups=near)

    updated = pl.pallas_call(
        update_kernel,
        in_specs=[inner] * 3,
        out_specs=outer,
        out_shape=jax.ShapeDtypeStruct((rows, width), bf16),
        scratch_shapes=[pltpu.VMEM((rows, width), bf16), pltpu.SemaphoreType.DMA((3,))],
        compiler_params=params(),
        name="update",
    )(solved, gain, arrived.reshape(width, WIDE))
    return updated[None, None, None]


def solution(mesh):
    return jax.shard_map(
        on_device,
        mesh=mesh,
        in_specs=(
            P("stream", "gy", "gz", None, None),
            P("stream", "gy", "gz", None, None),
            P("stream", "gy", "gz", None, None, None),
            P("stream", "gy", "gz", None, None),
            P("stream", "gy", "gz", None, None),
        ),
        out_specs=P("stream", "gy", "gz", None, None),
        check_vma=False,
    )
```
